32 devices in a mesh: frame: 8 (over y, x, core), tensor: 4 (over z).
Axes of the slice: x: 2, y: 2, z: 4, core: 2. Of those that a mesh axis runs over, the one named last changes fastest.
Arguments:
- queue_state: float32 [6144, 3072], P('frame', 'tensor'), may hold values from -6 to 6
- fresh_noise: float32 [768, 3072], P(None, 'tensor'), may hold values from -6 to 6
- levels: int32 [8], P('frame'), may hold values from 0 to 49
- reach_slot: int32 [8], P('frame'), may hold values from 1 to 3, as said below
- mod_table: float32 [50, 9216], replicated, may hold values from -3 to 3
- step_table: float32 [50], replicated, may hold values from -0.5 to -0.2
- norm_gain: float32 [2, 128], replicated, may hold values from 1 to 2.5
- input_weight: bfloat16 [3072, 3, 3072], P(None, None, 'tensor'), may hold values from -0.109375 to 0.109375
- output_weight: bfloat16 [3072, 3072], P('tensor'), may hold values from -0.109375 to 0.109375
Outputs:
- advanced: float32 [6144, 3072], P('frame', 'tensor')
The draws below stay inside these ranges and needn't reach their ends.
Inputs may be any that keep to these rules, and one draw needn't show every extreme that they name: `reach_slot`: some slot with index 3 or more attends to 3 frames on each side.
All inputs are finite; a program needn't handle non-finite values.
Results may differ from the reference program's by a relative error of at most 0.014.
Values may be sent and summed in bfloat16 or wider, within the bound.
No kernel may reach another device: no remote copies, remote signals or barrier semaphores. Data moves between devices by JAX's collectives and lax.ppermute only.
A program may use at most 192 MiB of HBM per device.

```python
import math
import jax
import jax.numpy as jnp
from jax import lax

D = 3072
HEADS = 24
HD = 128
TOK_FRAME = 768
LEVELS = 50
REACH = 3
STEPS = 2
FRAMES = 8
N_TENSOR = 4


def draw_reach_slot(key, part):
    key = jax.random.fold_in(key, 7)
    first_key, second_key = jax.random.split(key)
    base_draw = jax.random.randint(first_key, (FRAMES,), 1, REACH + 1)
    chosen_slot = jax.random.randint(second_key, (), REACH, FRAMES)
    return jnp.where(jnp.arange(FRAMES) == chosen_slot, REACH, base_draw).astype(jnp.int32)


def with_ends(entries, rng, low, largest):
    extent = entries.shape
    index_at = [jax.random.randint(jax.random.fold_in(rng, axis), (), 0, extent[axis]) for axis in range(len(extent))]
    entries = entries.at[tuple(index_at)].set(low)
    longest = extent.index(max(extent))
    index_at[longest] = (index_at[longest] + 1) % extent[longest]
    return entries.at[tuple(index_at)].set(largest)


def block_scale(stream_key, extent, cuts, least, high):
    loudness, own = 1.0, jax.random.fold_in(stream_key, 6)
    for dim, blocks in cuts:
        heights = jnp.exp(jax.random.uniform(jax.random.fold_in(own, dim), (blocks,), jnp.float32, least / len(cuts), high / len(cuts)))
        loudness = loudness * jnp.repeat(heights, extent[dim] // blocks).reshape([-1 if axis == dim else 1 for axis in range(len(extent))])
    return loudness


def normal_values(rng, dims, spread, limit, cuts=(), held_as=jnp.bfloat16):
    entries = jax.random.normal(rng, dims, jnp.float32) * spread
    if len(cuts) > 0:
        entries = block_scale(rng, dims, cuts, -0.22, 0.18) * entries
    return jnp.clip(entries, min=-limit, max=limit).astype(held_as)


def setup_inputs(seed: int = 0) -> dict:
    keys = jax.random.split(jax.random.key(seed), 10)
    queue_state = normal_values(keys[0], (FRAMES * TOK_FRAME, D), 1.0, 6.0, ((0, 8), (1, 4)), jnp.float32)
    fresh_noise = normal_values(keys[1], (TOK_FRAME, D), 1.0, 6.0, ((1, 4),), jnp.float32)
    levels = with_ends(jax.random.randint(keys[2], (FRAMES,), 0, LEVELS), jax.random.fold_in(keys[2], 1), 0, LEVELS - 1).astype(jnp.int32)
    reach_slot = draw_reach_slot(jax.random.fold_in(keys[9], 71), 0)
    mod_table = normal_values(keys[4], (LEVELS, 3 * D), 0.6, 3.0, (), jnp.float32)
    step_table = jnp.clip(jax.random.uniform(keys[5], (LEVELS,), jnp.float32, -0.5, -0.2), -0.5, -0.2)
    norm_gain = jnp.clip(jnp.exp(jax.random.uniform(keys[6], (2, HD), jnp.float32, math.log(1.0), math.log(2.5))), 1.0, 2.5)
    input_weight = normal_values(keys[7], (D, 3, D), D ** -0.5, 0.109375, ((2, 4),))
    output_weight = normal_values(keys[8], (D, D), D ** -0.5, 0.109375, ((0, 4),))
    return dict(queue_state=queue_state, fresh_noise=fresh_noise, levels=levels, reach_slot=reach_slot, mod_table=mod_table, step_table=step_table, norm_gain=norm_gain, input_weight=input_weight, output_weight=output_weight)


epsilon = 1e-06

def head_norm(values, gain):
    scale = lax.rsqrt(lax.optimization_barrier(jnp.mean(values * values, axis=-1, keepdims=True)) + epsilon)
    return values * scale * gain

def frame_inputs(latent_frame, shift_row, scale_row, input_weight, norm_gain):
    row_mean = lax.optimization_barrier(jnp.mean(latent_frame, axis=-1, keepdims=True))
    centered = latent_frame - row_mean
    row_var = lax.optimization_barrier(jnp.mean(centered * centered, axis=-1, keepdims=True))
    normed = (centered * lax.rsqrt(row_var + epsilon) * (1.0 + scale_row) + shift_row).astype(jnp.bfloat16)
    projected = jnp.dot(normed, input_weight.reshape(D, 3 * D), preferred_element_type=jnp.float32)
    projected = projected.reshape(TOK_FRAME, 3, HEADS, HD)
    queries = head_norm(projected[:, 0], norm_gain[0]).astype(jnp.bfloat16)
    key_block = head_norm(projected[:, 1], norm_gain[1]).astype(jnp.bfloat16)
    values = projected[:, 2].astype(jnp.bfloat16)
    return (queries, key_block, values)

def reference(queue_state, fresh_noise, levels, reach_slot, mod_table, step_table, norm_gain, input_weight, output_weight):
    latent = queue_state.reshape(FRAMES, TOK_FRAME, D)
    modulation = mod_table[levels]
    shift_rows = modulation[:, :D]
    scale_rows = modulation[:, D:2 * D]
    gate_rows = modulation[:, 2 * D:]
    step_size = step_table[levels]
    offsets = jnp.arange(-REACH, REACH + 1, dtype=jnp.int32)
    column_count = D // N_TENSOR
    advanced = latent
    for step_number in range(STEPS):
        if step_number > 0:
            latent = jnp.concatenate([fresh_noise[None], advanced[:-1]], axis=0)

        def prepare(items):
            return frame_inputs(items[0], items[1], items[2], input_weight, norm_gain)
        queries, key_block, values = lax.map(prepare, (latent, shift_rows, scale_rows))
        widths = ((REACH, REACH), (0, 0), (0, 0), (0, 0))
        padded_keys = jnp.pad(key_block, widths)
        padded_values = jnp.pad(values, widths)

        def attend(items):
            index, query_frame = items
            window_keys = lax.dynamic_slice_in_dim(padded_keys, index, 2 * REACH + 1, 0)
            window_values = lax.dynamic_slice_in_dim(padded_values, index, 2 * REACH + 1, 0)
            usable = (jnp.abs(offsets) <= reach_slot[index]) & (index + offsets >= 0) & (index + offsets < FRAMES)
            scores = jnp.einsum('qhd,wkhd->hqwk', query_frame.astype(jnp.float32), window_keys.astype(jnp.float32)) / jnp.sqrt(jnp.float32(HD))
            probs = jnp.where(usable[None, None, :, None], jnp.exp(scores), jnp.float32(0.0))
            weight_sum = lax.optimization_barrier(jnp.sum(probs, axis=(2, 3)))
            rounded = probs.astype(jnp.bfloat16).astype(jnp.float32)
            weighted = jnp.einsum('hqwk,wkhd->qhd', rounded, window_values.astype(jnp.float32))
            attended = (weighted / jnp.transpose(weight_sum)[:, :, None]).reshape(TOK_FRAME, D).astype(jnp.bfloat16)
            mixed = jnp.zeros((TOK_FRAME, D), jnp.float32)
            for group in range(N_TENSOR):
                head_term = jnp.dot(attended[:, group * column_count:(group + 1) * column_count], output_weight[group * column_count:(group + 1) * column_count], preferred_element_type=jnp.float32)
                mixed = mixed + lax.optimization_barrier(head_term.astype(jnp.bfloat16)).astype(jnp.float32)
            return mixed
        mixed = lax.map(attend, (jnp.arange(FRAMES, dtype=jnp.int32), queries))
        advanced = latent + step_size[:, None, None] * (latent + gate_rows[:, None, :] * mixed)
    return advanced.reshape(FRAMES * TOK_FRAME, D)
```

```python
import functools
import math

import jax
import jax.numpy as jnp
from jax import lax
from jax.experimental import pallas as pl
from jax.experimental.pallas import tpu as pltpu
from jax.sharding import PartitionSpec as P

STEPS = 2
QUAD = 4
CHUNKS = 3
TILE = 256
VMEM = 56 * 1024 * 1024

epsilon = 1e-06


def permute(block, axis, route):
    size = lax.axis_size(axis)
    pairs = [(i, j) for i, j in ((i, route(i)) for i in range(size)) if 0 <= j < size]
    return lax.ppermute(block, axis, pairs)


def ring(block):
    size = lax.axis_size("tensor")
    return permute(block, "tensor", lambda i: (i + 1) % size)


def qkv_kernel(parts, heads, head_dim, order_ref, gain_ref, *refs):
    inputs, weights = refs[:parts], refs[parts : 2 * parts]
    query_ref, pair_ref = refs[2 * parts :]
    step = pl.program_id(0)
    total = jnp.dot(inputs[0][...], weights[0][...], preferred_element_type=jnp.float32)
    for part in range(1, parts):
        total += jnp.dot(inputs[part][...], weights[part][...], preferred_element_type=jnp.float32)

    def normed(row, factor):
        pieces = []
        for head in range(heads):
            piece = total[:, head * head_dim : (head + 1) * head_dim]
            scale = lax.rsqrt(jnp.mean(piece * piece, axis=-1, keepdims=True) + epsilon)
            pieces.append((piece * scale * (gain_ref[row : row + 1, :] * factor)).astype(jnp.bfloat16))
        return jnp.concatenate(pieces, axis=1) if heads > 1 else pieces[0]

    @pl.when(step == 0)
    def _():
        pair_ref[...] = normed(1, 1.0)

    @pl.when(step == 1)
    def _():
        pair_ref[...] = total.astype(jnp.bfloat16)

    @pl.when(step == 2)
    def _():
        query_ref[...] = normed(0, math.log2(math.e) / math.sqrt(head_dim))


def project(inputs, weight, order, norm_gain):
    parts = len(inputs)
    rows, columns = inputs[0].shape
    head_dim = norm_gain.shape[1]

    def weight_spec(part):
        return pl.BlockSpec((None, columns, columns), lambda j, order: ((j + 1) % 3, order[part], 0))

    return pl.pallas_call(
        functools.partial(qkv_kernel, parts, columns // head_dim, head_dim),
        grid_spec=pltpu.PrefetchScalarGridSpec(
            num_scalar_prefetch=1,
            grid=(3,),
            in_specs=[pl.BlockSpec(norm_gain.shape, lambda j, order: (0, 0))]
            + [pl.BlockSpec((rows, columns), lambda j, order: (0, 0)) for _ in range(parts)]
            + [weight_spec(part) for part in range(parts)],
            out_specs=[
                pl.BlockSpec((rows, columns), lambda j, order: (0, 0)),
                pl.BlockSpec((rows, columns), lambda j, order: (0, jnp.minimum(j, 1))),
            ],
        ),
        out_shape=[
            jax.ShapeDtypeStruct((rows, columns), jnp.bfloat16),
            jax.ShapeDtypeStruct((rows, 2 * columns), jnp.bfloat16),
        ],
        compiler_params=pltpu.CompilerParams(vmem_limit_bytes=VMEM),
        cost_estimate=pl.CostEstimate(
            flops=2 * rows * columns * parts * 3 * columns,
            bytes_accessed=2 * (columns * parts * 3 * columns + rows * columns * (parts + 3)),
            transcendentals=0,
        ),
        name="qkv",
    )(order, norm_gain, *inputs, *([weight] * parts))


def attend_kernel(chunks, pieces, first, last, tile, usable_ref, *refs):
    queries, refs = refs[:chunks], refs[chunks:]
    keys, values = refs[:pieces], refs[pieces : 2 * pieces]
    rest = refs[2 * pieces :]
    total_in = None
    if not first:
        total_in, rest = rest[0], rest[1:]
    (out_ref,) = rest
    height, head_dim = queries[0].shape
    wide = []
    for piece in range(pieces):
        value = values[piece][...]
        usable = usable_ref[piece].astype(jnp.float32).astype(value.dtype)
        wide.append(jnp.concatenate([value, jnp.ones_like(value)], axis=1) * usable)
    for chunk in range(chunks):
        for start in range(0, height, tile):
            query = queries[chunk][start : start + tile, :]
            at = pl.ds(chunk * height + start, tile)
            total = None if first else total_in[at, :]
            for piece in range(pieces):
                scores = lax.dot_general(
                    query, keys[piece][...], (((1,), (1,)), ((), ())), preferred_element_type=jnp.float32
                )
                probs = jnp.exp2(scores).astype(jnp.bfloat16)
                added = jnp.dot(probs, wide[piece], preferred_element_type=jnp.float32)
                total = added if total is None else total + added
            if last:
                out_ref[at, :] = (total[:, :head_dim] / total[:, head_dim:]).astype(out_ref.dtype)
            else:
                out_ref[at, :] = total


def attend(queries, blocks, usable, running, last, head_dim):
    height, columns = queries[0].shape
    chunks = len(queries)
    rows = height * chunks
    heads = columns // head_dim
    pieces = len(blocks)
    first = running is None
    tile = TILE if height % TILE == 0 else height

    def key_spec(block):
        return pl.BlockSpec((block.shape[0], head_dim), lambda h, usable: (0, h))

    def value_spec(block):
        return pl.BlockSpec((block.shape[0], head_dim), lambda h, usable: (0, heads + h))

    running_spec = pl.BlockSpec((None, rows, 2 * head_dim), lambda h, usable: (h, 0, 0))
    key_rows = sum(block.shape[0] for block in blocks)
    return pl.pallas_call(
        functools.partial(attend_kernel, chunks, pieces, first, last, tile),
        grid_spec=pltpu.PrefetchScalarGridSpec(
            num_scalar_prefetch=1,
            grid=(heads,),
            in_specs=[pl.BlockSpec((height, head_dim), lambda h, usable: (0, h)) for _ in queries]
            + [key_spec(block) for block in blocks]
            + [value_spec(block) for block in blocks]
            + ([] if first else [running_spec]),
            out_specs=pl.BlockSpec((rows, head_dim), lambda h, usable: (0, h)) if last else running_spec,
        ),
        out_shape=jax.ShapeDtypeStruct((rows, columns), jnp.bfloat16)
        if last
        else jax.ShapeDtypeStruct((heads, rows, 2 * head_dim), jnp.float32),
        compiler_params=pltpu.CompilerParams(vmem_limit_bytes=VMEM),
        cost_estimate=pl.CostEstimate(
            flops=8 * rows * key_rows * columns,
            bytes_accessed=4 * key_rows * columns + 12 * rows * columns,
            transcendentals=rows * key_rows * heads,
        ),
        name="attend",
    )(usable, *queries, *blocks, *blocks, *([] if first else [running]))


def first_share_kernel(order_ref, attended_ref, weight_ref, *out_refs):
    share = jnp.dot(
        attended_ref[...], weight_ref[...], preferred_element_type=jnp.float32
    ).astype(jnp.bfloat16)
    height = out_refs[0].shape[0]
    for index, out_ref in enumerate(out_refs):
        out_ref[...] = share[index * height : (index + 1) * height]


def share_kernel(order_ref, attended_ref, weight_ref, out_ref):
    out_ref[...] = jnp.dot(
        attended_ref[...], weight_ref[...], preferred_element_type=jnp.float32
    ).astype(out_ref.dtype)


def shares(attended, weight, order, chunks):
    rows, depth = attended.shape
    count = order.shape[0]
    columns = weight.shape[1] // lax.axis_size("tensor")
    if chunks:
        kernel = first_share_kernel
        out_specs = [pl.BlockSpec((rows // chunks, columns), lambda j, order: (0, 0))] * chunks
        out_shape = [jax.ShapeDtypeStruct((rows // chunks, columns), jnp.bfloat16)] * chunks
    else:
        kernel = share_kernel
        out_specs = pl.BlockSpec((None, rows, columns), lambda j, order: (j, 0, 0))
        out_shape = jax.ShapeDtypeStruct((count, rows, columns), jnp.bfloat16)
    return pl.pallas_call(
        kernel,
        grid_spec=pltpu.PrefetchScalarGridSpec(
            num_scalar_prefetch=1,
            grid=(count,),
            in_specs=[
                pl.BlockSpec((rows, depth), lambda j, order: (0, 0)),
                pl.BlockSpec((depth, columns), lambda j, order: (0, order[j])),
            ],
            out_specs=out_specs,
        ),
        out_shape=out_shape,
        compiler_params=pltpu.CompilerParams(vmem_limit_bytes=VMEM),
        cost_estimate=pl.CostEstimate(
            flops=2 * rows * depth * columns * count,
            bytes_accessed=2 * (rows * depth + count * columns * (rows + depth)),
            transcendentals=0,
        ),
        name="shares",
    )(order, attended, weight)


def summed(block):
    size = lax.axis_size("tensor")
    total = block
    for distance in range(1, size):
        total = total + permute(block, "tensor", lambda i: (i + distance) % size)
    return total


def sums_of(block):
    return jnp.stack([jnp.sum(block, axis=1), jnp.sum(block * block, axis=1)])


def chunk_sums(sums, index, height):
    return sums[:, index * height : (index + 1) * height]


def normalize(block, sums, full_width, shift, scale):
    mean = sums[0] / full_width
    var = sums[1] / full_width - mean * mean
    return (
        (block - mean[:, None]) * lax.rsqrt(var + epsilon)[:, None] * (1.0 + scale) + shift
    ).astype(jnp.bfloat16)


def sibling(block):
    return permute(block, "frame", lambda i: i ^ 1)


def halo(pair):
    across = permute(pair, "frame", lambda i: i ^ 2)
    near = sibling(pair)
    third = permute(pair, "frame", lambda i: i + (3 if i % 2 else -3))
    second = permute(across, "frame", lambda i: i + (QUAD if i % QUAD < 2 else -QUAD))
    return dict(
        own=pair, near=near, across=across, beyond=sibling(across), third=third, second=second, other=sibling(second)
    )


SOURCES = ("own", "near", "across", "beyond", "third", "second", "other")


def usable_sources(slot, frames, reach):
    place = slot % QUAD
    held = dict(
        own=slot,
        near=slot ^ 1,
        across=slot ^ 2,
        beyond=slot ^ 3,
        third=jnp.where(place % 2 == 0, slot - 3, slot + 3),
        second=jnp.where(place < 2, slot - 2, slot + 2),
        other=slot + jnp.where(place == 0, -1, jnp.where(place == 1, -3, jnp.where(place == 2, 3, 1))),
    )
    return {
        name: ((jnp.abs(g - slot) <= reach) & (g >= 0) & (g < frames)).astype(jnp.int32) for name, g in held.items()
    }


def on_device(
    queue_state,
    fresh_noise,
    levels,
    reach_slot,
    mod_table,
    step_table,
    norm_gain,
    input_weight,
    output_weight,
):
    rows, columns = queue_state.shape
    tensor_count = lax.axis_size("tensor")
    full_width = columns * tensor_count
    frames = lax.axis_size("frame")
    slot = lax.axis_index("frame")
    place = lax.axis_index("tensor")
    head_dim = norm_gain.shape[1]
    height = rows // CHUNKS

    def pieces_of(vector_level):
        row = lax.dynamic_index_in_dim(mod_table, vector_level, 0, keepdims=False)
        return [
            lax.dynamic_slice_in_dim(row, part * full_width + place * columns, columns) for part in range(3)
        ]

    level = levels[0]
    shift, scale, gate = pieces_of(level)
    step_size = lax.dynamic_index_in_dim(step_table, level, 0, keepdims=False)
    next_level = permute(levels, "frame", lambda i: i - 1)[0]
    next_shift, next_scale, _ = pieces_of(next_level)
    usable = usable_sources(slot, frames, reach_slot[0])
    gather_order = (place - jnp.arange(tensor_count, dtype=jnp.int32)) % tensor_count
    scatter_order = (place - 1 - jnp.arange(tensor_count, dtype=jnp.int32)) % tensor_count
    weights = jnp.transpose(input_weight, (1, 0, 2))

    def chunk(array, index):
        return array[index * height : (index + 1) * height]

    first_sums = summed(jnp.concatenate([sums_of(queue_state), sums_of(fresh_noise)]))
    normed = [
        normalize(chunk(queue_state, i), chunk_sums(first_sums[:2], i, height), full_width, shift, scale)
        for i in range(CHUNKS)
    ]
    latents = [chunk(queue_state, i) for i in range(CHUNKS)]
    fresh_normed = normalize(fresh_noise, first_sums[2:], full_width, shift, scale)
    advanced = None

    for step_number in range(STEPS):
        queries, sources = [], []
        waiting = None
        for i in range(CHUNKS):
            own = normed[i]
            if waiting is not None:
                gathered_before, own = lax.optimization_barrier((waiting[-1], own))
                waiting[-1] = gathered_before
                waiting.append(ring(waiting[-1]))
                query, pair = project(waiting, weights, gather_order, norm_gain)
                queries.append(query)
                sources.append(halo(pair))
            waiting = [own]
            for _ in range(tensor_count - 2):
                waiting.append(ring(waiting[-1]))
        waiting.append(ring(waiting[-1]))
        query, pair = project(waiting, weights, gather_order, norm_gain)
        queries.append(query)
        sources.append(halo(pair))

        def flags(names):
            return jnp.stack([usable[name] for _, name in names])

        final = CHUNKS - 1
        late_names = ("second", "other")
        early = [(i, name) for i in range(final - 1) for name in SOURCES]
        early += [(final - 1, name) for name in SOURCES if name not in late_names]
        middle = [(final - 1, name) for name in late_names]
        middle += [(final, name) for name in SOURCES if name not in late_names]
        late = [(final, name) for name in late_names]
        running = None
        for names in (early, middle, late):
            running = attend(
                queries,
                [sources[i][name] for i, name in names],
                flags(names),
                running,
                names is late,
                head_dim,
            )

        if step_number > 0:
            advanced, running = lax.optimization_barrier((advanced, running))
            moved = [permute(done, "frame", lambda i: i + 1) for done in advanced]
            latents = [jnp.where(slot == 0, chunk(fresh_noise, j), moved[j]) for j in range(CHUNKS)]

        totals = list(shares(running, output_weight, scatter_order[:1], CHUNKS))
        others = shares(running, output_weight, scatter_order[1:], 0)
        for hop in range(tensor_count - 1):
            for j in range(CHUNKS):
                total = ring(totals[j]).astype(jnp.float32) + chunk(others[hop], j).astype(jnp.float32)
                totals[j] = total.astype(jnp.bfloat16) if hop < tensor_count - 2 else total
        advanced = [
            latents[j] + step_size * (latents[j] + gate * totals[j]) for j in range(CHUNKS)
        ]
        if step_number < STEPS - 1:
            normed = []
            for j in range(CHUNKS):
                sums = summed(sums_of(advanced[j]))
                ready = permute(
                    normalize(advanced[j], sums, full_width, next_shift, next_scale), "frame", lambda i: i + 1
                )
                normed.append(jnp.where(slot == 0, chunk(fresh_normed, j), ready))
    return jnp.concatenate(advanced, axis=0)


def solution(mesh):
    return jax.shard_map(
        on_device,
        mesh=mesh,
        in_specs=(
            P("frame", "tensor"),
            P(None, "tensor"),
            P("frame"),
            P("frame"),
            P(),
            P(),
            P(),
            P(None, None, "tensor"),
            P("tensor", None),
        ),
        out_specs=P("frame", "tensor"),
        check_vma=False,
    )
```

```python
import functools
import math

import jax
import jax.numpy as jnp
from jax import lax
from jax.experimental import pallas as pl
from jax.experimental.pallas import tpu as pltpu
from jax.sharding import PartitionSpec as P

STEPS = 2
QUAD = 4
CHUNKS = 3
TILE = 256
VMEM = 56 * 1024 * 1024

epsilon = 1e-06
QUICK = pl.CostEstimate(flops=1000, bytes_accessed=1000, transcendentals=0)


def permute(block, axis, route):
    size = lax.axis_size(axis)
    pairs = [(i, j) for i, j in ((i, route(i)) for i in range(size)) if 0 <= j < size]
    return lax.ppermute(block, axis, pairs)


def ring(block):
    size = lax.axis_size("tensor")
    return permute(block, "tensor", lambda i: (i + 1) % size)


def qkv_kernel(parts, heads, head_dim, order_ref, gain_ref, *refs):
    inputs, weights = refs[:parts], refs[parts : 2 * parts]
    query_ref, pair_ref = refs[2 * parts :]
    step = pl.program_id(0)
    total = jnp.dot(inputs[0][...], weights[0][...], preferred_element_type=jnp.float32)
    for part in range(1, parts):
        total += jnp.dot(inputs[part][...], weights[part][...], preferred_element_type=jnp.float32)

    def normed(row, factor):
        pieces = []
        for head in range(heads):
            piece = total[:, head * head_dim : (head + 1) * head_dim]
            scale = lax.rsqrt(jnp.mean(piece * piece, axis=-1, keepdims=True) + epsilon)
            pieces.append((piece * scale * (gain_ref[row : row + 1, :] * factor)).astype(jnp.bfloat16))
        return jnp.concatenate(pieces, axis=1) if heads > 1 else pieces[0]

    @pl.when(step == 0)
    def _():
        pair_ref[...] = normed(1, 1.0)

    @pl.when(step == 1)
    def _():
        pair_ref[...] = total.astype(jnp.bfloat16)

    @pl.when(step == 2)
    def _():
        query_ref[...] = normed(0, math.log2(math.e) / math.sqrt(head_dim))


def project(inputs, weight, order, norm_gain):
    parts = len(inputs)
    rows, columns = inputs[0].shape
    head_dim = norm_gain.shape[1]

    def weight_spec(part):
        return pl.BlockSpec((None, columns, columns), lambda j, order: ((j + 1) % 3, order[part], 0))

    return pl.pallas_call(
        functools.partial(qkv_kernel, parts, columns // head_dim, head_dim),
        grid_spec=pltpu.PrefetchScalarGridSpec(
            num_scalar_prefetch=1,
            grid=(3,),
            in_specs=[pl.BlockSpec(norm_gain.shape, lambda j, order: (0, 0))]
            + [pl.BlockSpec((rows, columns), lambda j, order: (0, 0)) for _ in range(parts)]
            + [weight_spec(part) for part in range(parts)],
            out_specs=[
                pl.BlockSpec((rows, columns), lambda j, order: (0, 0)),
                pl.BlockSpec((rows, columns), lambda j, order: (0, jnp.minimum(j, 1))),
            ],
        ),
        out_shape=[
            jax.ShapeDtypeStruct((rows, columns), jnp.bfloat16),
            jax.ShapeDtypeStruct((rows, 2 * columns), jnp.bfloat16),
        ],
        compiler_params=pltpu.CompilerParams(vmem_limit_bytes=VMEM),
        cost_estimate=QUICK,
        name="qkv",
    )(order, norm_gain, *inputs, *([weight] * parts))


def attend_kernel(chunks, pieces, first, last, tile, usable_ref, *refs):
    queries, refs = refs[:chunks], refs[chunks:]
    keys, values = refs[:pieces], refs[pieces : 2 * pieces]
    rest = refs[2 * pieces :]
    total_in = None
    if not first:
        total_in, rest = rest[0], rest[1:]
    (out_ref,) = rest
    height, head_dim = queries[0].shape
    wide = []
    for piece in range(pieces):
        value = values[piece][...]
        usable = usable_ref[piece].astype(jnp.float32).astype(value.dtype)
        wide.append(jnp.concatenate([value, jnp.ones_like(value)], axis=1) * usable)
    for chunk in range(chunks):
        for start in range(0, height, tile):
            query = queries[chunk][start : start + tile, :]
            at = pl.ds(chunk * height + start, tile)
            total = None if first else total_in[at, :]
            for piece in range(pieces):
                scores = lax.dot_general(
                    query, keys[piece][...], (((1,), (1,)), ((), ())), preferred_element_type=jnp.float32
                )
                probs = jnp.exp2(scores).astype(jnp.bfloat16)
                added = jnp.dot(probs, wide[piece], preferred_element_type=jnp.float32)
                total = added if total is None else total + added
            if last:
                out_ref[at, :] = (total[:, :head_dim] / total[:, head_dim:]).astype(out_ref.dtype)
            else:
                out_ref[at, :] = total


def attend(queries, blocks, parts, usable, running, last, head_dim):
    height, columns = queries[0].shape
    chunks = len(queries)
    rows = height * chunks
    heads = columns // head_dim
    pieces = len(blocks)
    first = running is None
    tile = TILE if height % TILE == 0 else height

    def key_spec(part):
        return pl.BlockSpec((height, head_dim), lambda h, usable: (part, h))

    def value_spec(part):
        return pl.BlockSpec((height, head_dim), lambda h, usable: (part, heads + h))

    running_spec = pl.BlockSpec((None, rows, 2 * head_dim), lambda h, usable: (h, 0, 0))
    return pl.pallas_call(
        functools.partial(attend_kernel, chunks, pieces, first, last, tile),
        grid_spec=pltpu.PrefetchScalarGridSpec(
            num_scalar_prefetch=1,
            grid=(heads,),
            in_specs=[pl.BlockSpec((height, head_dim), lambda h, usable: (0, h)) for _ in queries]
            + [key_spec(part) for part in parts]
            + [value_spec(part) for part in parts]
            + ([] if first else [running_spec]),
            out_specs=pl.BlockSpec((rows, head_dim), lambda h, usable: (0, h)) if last else running_spec,
        ),
        out_shape=jax.ShapeDtypeStruct((rows, columns), jnp.bfloat16)
        if last
        else jax.ShapeDtypeStruct((heads, rows, 2 * head_dim), jnp.float32),
        compiler_params=pltpu.CompilerParams(vmem_limit_bytes=VMEM),
        cost_estimate=QUICK,
        name="attend",
    )(usable, *queries, *blocks, *blocks, *([] if first else [running]))


def first_share_kernel(order_ref, attended_ref, weight_ref, *out_refs):
    share = jnp.dot(
        attended_ref[...], weight_ref[...], preferred_element_type=jnp.float32
    ).astype(jnp.bfloat16)
    height = out_refs[0].shape[0]
    for index, out_ref in enumerate(out_refs):
        out_ref[...] = share[index * height : (index + 1) * height]


def share_kernel(order_ref, attended_ref, weight_ref, out_ref):
    out_ref[...] = jnp.dot(
        attended_ref[...], weight_ref[...], preferred_element_type=jnp.float32
    ).astype(out_ref.dtype)


def shares(attended, weight, order, chunks):
    rows, depth = attended.shape
    count = order.shape[0]
    columns = weight.shape[1] // lax.axis_size("tensor")
    if chunks:
        kernel = first_share_kernel
        out_specs = [pl.BlockSpec((rows // chunks, columns), lambda j, order: (0, 0))] * chunks
        out_shape = [jax.ShapeDtypeStruct((rows // chunks, columns), jnp.bfloat16)] * chunks
    else:
        kernel = share_kernel
        out_specs = pl.BlockSpec((None, rows, columns), lambda j, order: (j, 0, 0))
        out_shape = jax.ShapeDtypeStruct((count, rows, columns), jnp.bfloat16)
    return pl.pallas_call(
        kernel,
        grid_spec=pltpu.PrefetchScalarGridSpec(
            num_scalar_prefetch=1,
            grid=(count,),
            in_specs=[
                pl.BlockSpec((rows, depth), lambda j, order: (0, 0)),
                pl.BlockSpec((depth, columns), lambda j, order: (0, order[j])),
            ],
            out_specs=out_specs,
        ),
        out_shape=out_shape,
        compiler_params=pltpu.CompilerParams(vmem_limit_bytes=VMEM),
        cost_estimate=QUICK,
        name="shares",
    )(order, attended, weight)


def add_kernel(total_ref, share_ref, out_ref):
    out_ref[...] = (total_ref[...].astype(jnp.float32) + share_ref[...].astype(jnp.float32)).astype(out_ref.dtype)


def add_share(total, others, hop, index, dtype):
    rows, columns = total.shape
    return pl.pallas_call(
        add_kernel,
        grid=(1,),
        in_specs=[
            pl.BlockSpec((rows, columns), lambda j: (0, 0)),
            pl.BlockSpec((None, rows, columns), lambda j: (hop, index, 0)),
        ],
        out_specs=pl.BlockSpec((rows, columns), lambda j: (0, 0)),
        out_shape=jax.ShapeDtypeStruct((rows, columns), dtype),
        compiler_params=pltpu.CompilerParams(vmem_limit_bytes=VMEM),
        cost_estimate=QUICK,
        name="add_share",
    )(total, others)


def turn_kernel(full_width, leaves_ref, total_ref, share_ref, latent_ref, fresh_ref, rows_ref, out_ref, sums_ref):
    total = total_ref[...].astype(jnp.float32) + share_ref[...].astype(jnp.float32)
    latent = latent_ref[...]
    advanced = latent + rows_ref[1:2, :] * (latent + rows_ref[0:1, :] * total)
    kept = jnp.where(leaves_ref[0] != 0, fresh_ref[...], advanced)
    out_ref[...] = kept
    lane = lax.broadcasted_iota(jnp.int32, (kept.shape[0], 128), 1)
    first = jnp.sum(kept, axis=1, keepdims=True)
    second = jnp.sum(kept * kept, axis=1, keepdims=True)
    both = jnp.where(lane == 0, first, jnp.where(lane == 1, second, 0.0))
    sums_ref[...] = jnp.transpose(both)[: sums_ref.shape[0]]


def turn(total, others, hop, index, latent, fresh, rows, leaves, full_width):
    height, columns = total.shape
    whole = pl.BlockSpec((height, columns), lambda j, leaves: (0, 0))
    return pl.pallas_call(
        functools.partial(turn_kernel, full_width),
        grid_spec=pltpu.PrefetchScalarGridSpec(
            num_scalar_prefetch=1,
            grid=(1,),
            in_specs=[
                whole,
                pl.BlockSpec((None, height, columns), lambda j, leaves: (hop, index, 0)),
                pl.BlockSpec((height, columns), lambda j, leaves: (index, 0)),
                pl.BlockSpec((height, columns), lambda j, leaves: (index, 0)),
                pl.BlockSpec((2, columns), lambda j, leaves: (0, 0)),
            ],
            out_specs=[whole, pl.BlockSpec((8, height), lambda j, leaves: (0, 0))],
        ),
        out_shape=[
            jax.ShapeDtypeStruct((height, columns), jnp.float32),
            jax.ShapeDtypeStruct((8, height), jnp.float32),
        ],
        compiler_params=pltpu.CompilerParams(vmem_limit_bytes=VMEM),
        cost_estimate=QUICK,
        name="turn",
    )(leaves, total, others, latent, fresh, rows)


def normalize_kernel(full_width, count, block_ref, rows_ref, *refs):
    sums = refs[0][...]
    for part in range(1, count):
        sums = sums + refs[part][...]
    upright = jnp.transpose(sums)
    mean = upright[:, 0:1] / full_width
    var = upright[:, 1:2] / full_width - mean * mean
    out_ref = refs[count]
    out_ref[...] = (
        (block_ref[...] - mean) * lax.rsqrt(var + epsilon) * (1.0 + rows_ref[1:2, :]) + rows_ref[0:1, :]
    ).astype(out_ref.dtype)


def normalize_turned(block, sums, rows, full_width):
    size = lax.axis_size("tensor")
    everyone = [sums]
    for distance in range(1, size):
        everyone.append(permute(sums, "tensor", lambda i: (i + distance) % size))
    return pl.pallas_call(
        functools.partial(normalize_kernel, full_width, size),
        out_shape=jax.ShapeDtypeStruct(block.shape, jnp.bfloat16),
        compiler_params=pltpu.CompilerParams(vmem_limit_bytes=VMEM),
        cost_estimate=QUICK,
        name="normalize",
    )(block, rows, *everyone)


def onward(block):
    size = lax.axis_size("frame")
    return permute(block, "frame", lambda i: (i + 1) % size)


def summed(block):
    size = lax.axis_size("tensor")
    total = block
    for distance in range(1, size):
        total = total + permute(block, "tensor", lambda i: (i + distance) % size)
    return total


def sums_of(block):
    return jnp.stack([jnp.sum(block, axis=1), jnp.sum(block * block, axis=1)])


def chunk_sums(sums, index, height):
    return sums[:, index * height : (index + 1) * height]


def normalize(block, sums, full_width, shift, scale):
    mean = sums[0] / full_width
    var = sums[1] / full_width - mean * mean
    return (
        (block - mean[:, None]) * lax.rsqrt(var + epsilon)[:, None] * (1.0 + scale) + shift
    ).astype(jnp.bfloat16)


def sibling(block):
    return permute(block, "frame", lambda i: i ^ 1)


def halo(pair):
    return dict(
        own=pair,
        across=permute(pair, "frame", lambda i: i ^ 2),
        third=permute(pair, "frame", lambda i: i + (3 if i % 2 else -3)),
    )


def halo_second(held):
    held["second"] = permute(held["across"], "frame", lambda i: i + (QUAD if i % QUAD < 2 else -QUAD))


def halo_sibling(held):
    held["sibling"] = sibling(jnp.concatenate([held["own"], held["across"], held["second"]]))


SIBLING = dict(near=0, beyond=1, other=2)


def tie(*arrays):
    return lax.optimization_barrier(arrays)


SOURCES = ("own", "near", "across", "beyond", "third", "second", "other")


def usable_sources(slot, frames, reach):
    place = slot % QUAD
    held = dict(
        own=slot,
        near=slot ^ 1,
        across=slot ^ 2,
        beyond=slot ^ 3,
        third=jnp.where(place % 2 == 0, slot - 3, slot + 3),
        second=jnp.where(place < 2, slot - 2, slot + 2),
        other=slot + jnp.where(place == 0, -1, jnp.where(place == 1, -3, jnp.where(place == 2, 3, 1))),
    )
    return {
        name: ((jnp.abs(g - slot) <= reach) & (g >= 0) & (g < frames)).astype(jnp.int32) for name, g in held.items()
    }


def on_device(
    queue_state,
    fresh_noise,
    levels,
    reach_slot,
    mod_table,
    step_table,
    norm_gain,
    input_weight,
    output_weight,
):
    rows, columns = queue_state.shape
    tensor_count = lax.axis_size("tensor")
    full_width = columns * tensor_count
    frames = lax.axis_size("frame")
    slot = lax.axis_index("frame")
    place = lax.axis_index("tensor")
    head_dim = norm_gain.shape[1]
    height = rows // CHUNKS

    def pieces_of(vector_level):
        row = lax.dynamic_index_in_dim(mod_table, vector_level, 0, keepdims=False)
        return [
            lax.dynamic_slice_in_dim(row, part * full_width + place * columns, columns) for part in range(3)
        ]

    level = levels[0]
    shift, scale, gate = pieces_of(level)
    step_size = lax.dynamic_index_in_dim(step_table, level, 0, keepdims=False)
    next_level = permute(levels, "frame", lambda i: (i - 1) % frames)[0]
    next_rows = jnp.stack(pieces_of(next_level)[:2])
    update_rows = jnp.stack([gate, jnp.full_like(gate, step_size)])
    leaves = (slot == frames - 1).astype(jnp.int32).reshape(1)
    usable = usable_sources(slot, frames, reach_slot[0])
    gather_order = (place - jnp.arange(tensor_count, dtype=jnp.int32)) % tensor_count
    scatter_order = (place - 1 - jnp.arange(tensor_count, dtype=jnp.int32)) % tensor_count
    weights = jnp.transpose(input_weight, (1, 0, 2))

    def chunk(array, index):
        return array[index * height : (index + 1) * height]

    first_sums = summed(sums_of(queue_state))
    normed = [
        normalize(chunk(queue_state, i), chunk_sums(first_sums, i, height), full_width, shift, scale)
        for i in range(CHUNKS)
    ]
    latents = None
    kept = None

    for step_number in range(STEPS):
        queries, sources = [], []
        gathered = [normed[0]]
        for _ in range(tensor_count - 2):
            gathered.append(ring(gathered[-1]))
        for i in range(CHUNKS):
            if i > 0:
                gathered[-1], sources[-1]["own"] = tie(gathered[-1], sources[-1]["own"])
            following = None
            if i + 1 < CHUNKS:
                gathered[-1], own = tie(gathered[-1], normed[i + 1])
                last, arrived = tie(ring(gathered[-1]), ring(own))
                following = [own, arrived]
                for _ in range(tensor_count - 3):
                    following.append(ring(following[-1]))
            else:
                last = ring(gathered[-1])
            if i > 1:
                last, sources[-2]["second"] = tie(last, sources[-2]["second"])
                halo_sibling(sources[-2])
            if 0 < i < CHUNKS - 1:
                last, sources[-1]["across"] = tie(last, sources[-1]["across"])
                halo_second(sources[-1])
            query, pair = project(gathered + [last], weights, gather_order, norm_gain)
            queries.append(query)
            sources.append(halo(pair))
            gathered = following
        final = CHUNKS - 1
        early = [(i, name) for i in range(final - 1) for name in SOURCES]
        early += [(final - 1, name) for name in ("own", "across", "third")] + [(final, "own")]
        middle = [(final - 1, "second"), (final, "across"), (final, "third")]
        middle += [(final - 1, name) for name in SIBLING]
        late = [(final, "second")] + [(final, name) for name in SIBLING]

        def absorb(names, running, last):
            return attend(
                queries,
                [sources[i]["sibling" if name in SIBLING else name] for i, name in names],
                [SIBLING.get(name, 0) for _, name in names],
                jnp.stack([usable[name] for _, name in names]),
                running,
                last,
                head_dim,
            )

        before, after = sources[-2], sources[-1]
        queries[-1], before["across"] = tie(queries[-1], before["across"])
        halo_second(before)
        running = absorb(early, None, False)
        running, before["second"], after["across"] = tie(running, before["second"], after["across"])
        halo_second(after)
        halo_sibling(before)
        running = absorb(middle, running, False)
        running, after["second"] = tie(running, after["second"])
        halo_sibling(after)
        running = absorb(late, running, True)

        if step_number > 0:
            kept, running = tie(kept, running)
            latents = [onward(block) for block in kept]

        totals = list(shares(running, output_weight, scatter_order[:1], CHUNKS))
        others = shares(running, output_weight, scatter_order[1:], 0)
        turning = step_number < STEPS - 1
        for hop in range(tensor_count - 1):
            last = hop == tensor_count - 2
            for j in range(CHUNKS):
                totals[j] = ring(totals[j])
                if not (last and turning):
                    totals[j] = add_share(totals[j], others, hop, j, jnp.float32 if last else jnp.bfloat16)
        if turning:
            kept, normed = [], []
            for j in range(CHUNKS):
                block, sums = turn(
                    totals[j],
                    others,
                    tensor_count - 2,
                    j,
                    queue_state,
                    fresh_noise,
                    update_rows,
                    leaves,
                    full_width,
                )
                kept.append(block)
                normed.append(onward(normalize_turned(block, sums, next_rows, full_width)))
    advanced = [latents[j] + step_size * (latents[j] + gate * totals[j]) for j in range(CHUNKS)]
    return jnp.concatenate(advanced, axis=0)


def solution(mesh):
    return jax.shard_map(
        on_device,
        mesh=mesh,
        in_specs=(
            P("frame", "tensor"),
            P(None, "tensor"),
            P("frame"),
            P("frame"),
            P(),
            P(),
            P(),
            P(None, None, "tensor"),
            P("tensor", None),
        ),
        out_specs=P("frame", "tensor"),
        check_vma=False,
    )
```

```python
import functools
import math

import jax
import jax.numpy as jnp
from jax import lax
from jax.experimental import pallas as pl
from jax.experimental.pallas import tpu as pltpu
from jax.sharding import PartitionSpec as P

STEPS = 2
QUAD = 4
CHUNKS = 3
TILE = 256
VMEM = 56 * 1024 * 1024

epsilon = 1e-06
QUICK = pl.CostEstimate(flops=1000, bytes_accessed=1000, transcendentals=0)


def permute(block, axis, route):
    size = lax.axis_size(axis)
    pairs = [(i, j) for i, j in ((i, route(i)) for i in range(size)) if 0 <= j < size]
    return lax.ppermute(block, axis, pairs)


def ring(block):
    size = lax.axis_size("tensor")
    return permute(block, "tensor", lambda i: (i + 1) % size)


def qkv_kernel(parts, heads, head_dim, order_ref, gain_ref, *refs):
    inputs, weights = refs[:parts], refs[parts : 2 * parts]
    query_ref, pair_ref = refs[2 * parts :]
    step = pl.program_id(0)
    total = jnp.dot(inputs[0][...], weights[0][...], preferred_element_type=jnp.float32)
    for part in range(1, parts):
        total += jnp.dot(inputs[part][...], weights[part][...], preferred_element_type=jnp.float32)

    def normed(row, factor):
        pieces = []
        for head in range(heads):
            piece = total[:, head * head_dim : (head + 1) * head_dim]
            scale = lax.rsqrt(jnp.mean(piece * piece, axis=-1, keepdims=True) + epsilon)
            pieces.append((piece * scale * (gain_ref[row : row + 1, :] * factor)).astype(jnp.bfloat16))
        return jnp.concatenate(pieces, axis=1) if heads > 1 else pieces[0]

    @pl.when(step == 0)
    def _():
        pair_ref[...] = normed(1, 1.0)

    @pl.when(step == 1)
    def _():
        pair_ref[...] = total.astype(jnp.bfloat16)

    @pl.when(step == 2)
    def _():
        query_ref[...] = normed(0, math.log2(math.e) / math.sqrt(head_dim))


def project(inputs, weight, order, norm_gain):
    parts = len(inputs)
    rows, columns = inputs[0].shape
    head_dim = norm_gain.shape[1]

    def weight_spec(part):
        return pl.BlockSpec((None, columns, columns), lambda j, order: ((j + 1) % 3, order[part], 0))

    return pl.pallas_call(
        functools.partial(qkv_kernel, parts, columns // head_dim, head_dim),
        grid_spec=pltpu.PrefetchScalarGridSpec(
            num_scalar_prefetch=1,
            grid=(3,),
            in_specs=[pl.BlockSpec(norm_gain.shape, lambda j, order: (0, 0))]
            + [pl.BlockSpec((rows, columns), lambda j, order: (0, 0)) for _ in range(parts)]
            + [weight_spec(part) for part in range(parts)],
            out_specs=[
                pl.BlockSpec((rows, columns), lambda j, order: (0, 0)),
                pl.BlockSpec((rows, columns), lambda j, order: (0, jnp.minimum(j, 1))),
            ],
        ),
        out_shape=[
            jax.ShapeDtypeStruct((rows, columns), jnp.bfloat16),
            jax.ShapeDtypeStruct((rows, 2 * columns), jnp.bfloat16),
        ],
        compiler_params=pltpu.CompilerParams(vmem_limit_bytes=VMEM),
        cost_estimate=QUICK,
        name="qkv",
    )(order, norm_gain, *inputs, *([weight] * parts))


def attend_kernel(chunks, marks, first, last, tile, usable_ref, *refs):
    pieces = len(marks)
    queries, refs = refs[:chunks], refs[chunks:]
    keys, values = refs[:pieces], refs[pieces : 2 * pieces]
    rest = refs[2 * pieces :]
    total_in = None
    if not first:
        total_in, rest = rest[0], rest[1:]
    (out_ref,) = rest
    height, head_dim = queries[0].shape
    wide = []
    for piece in range(pieces):
        value = values[piece][...]
        usable = usable_ref[marks[piece]].astype(jnp.float32).astype(value.dtype)
        wide.append(jnp.concatenate([value, jnp.ones_like(value)], axis=1) * usable)
    for chunk in range(chunks):
        for start in range(0, height, tile):
            query = queries[chunk][start : start + tile, :]
            at = pl.ds(chunk * height + start, tile)
            total = None if first else total_in[at, :]
            for piece in range(pieces):
                scores = lax.dot_general(
                    query, keys[piece][...], (((1,), (1,)), ((), ())), preferred_element_type=jnp.float32
                )
                probs = jnp.exp2(scores).astype(jnp.bfloat16)
                added = jnp.dot(probs, wide[piece], preferred_element_type=jnp.float32)
                total = added if total is None else total + added
            if last:
                out_ref[at, :] = (total[:, :head_dim] / total[:, head_dim:]).astype(out_ref.dtype)
            else:
                out_ref[at, :] = total


def attend(queries, blocks, parts, marks, usable, running, last, head_dim):
    height, columns = queries[0].shape
    chunks = len(queries)
    rows = height * chunks
    heads = columns // head_dim
    first = running is None
    tile = TILE if height % TILE == 0 else height

    def key_spec(part):
        return pl.BlockSpec((height, head_dim), lambda h, usable: (part, h))

    def value_spec(part):
        return pl.BlockSpec((height, head_dim), lambda h, usable: (part, heads + h))

    running_spec = pl.BlockSpec((None, rows, 2 * head_dim), lambda h, usable: (h, 0, 0))
    return pl.pallas_call(
        functools.partial(attend_kernel, chunks, marks, first, last, tile),
        grid_spec=pltpu.PrefetchScalarGridSpec(
            num_scalar_prefetch=1,
            grid=(heads,),
            in_specs=[pl.BlockSpec((height, head_dim), lambda h, usable: (0, h)) for _ in queries]
            + [key_spec(part) for part in parts]
            + [value_spec(part) for part in parts]
            + ([] if first else [running_spec]),
            out_specs=pl.BlockSpec((rows, head_dim), lambda h, usable: (0, h)) if last else running_spec,
        ),
        out_shape=jax.ShapeDtypeStruct((rows, columns), jnp.bfloat16)
        if last
        else jax.ShapeDtypeStruct((heads, rows, 2 * head_dim), jnp.float32),
        compiler_params=pltpu.CompilerParams(vmem_limit_bytes=VMEM),
        cost_estimate=QUICK,
        name="attend",
    )(usable, *queries, *blocks, *blocks, *([] if first else [running]))


def first_share_kernel(order_ref, attended_ref, weight_ref, *out_refs):
    share = jnp.dot(
        attended_ref[...], weight_ref[...], preferred_element_type=jnp.float32
    ).astype(jnp.bfloat16)
    height = out_refs[0].shape[0]
    for index, out_ref in enumerate(out_refs):
        out_ref[...] = share[index * height : (index + 1) * height]


def share_kernel(order_ref, attended_ref, weight_ref, out_ref):
    out_ref[...] = jnp.dot(
        attended_ref[...], weight_ref[...], preferred_element_type=jnp.float32
    ).astype(out_ref.dtype)


def shares(attended, weight, order, chunks):
    rows, depth = attended.shape
    count = order.shape[0]
    columns = weight.shape[1] // lax.axis_size("tensor")
    if chunks:
        kernel = first_share_kernel
        out_specs = [pl.BlockSpec((rows // chunks, columns), lambda j, order: (0, 0))] * chunks
        out_shape = [jax.ShapeDtypeStruct((rows // chunks, columns), jnp.bfloat16)] * chunks
    else:
        kernel = share_kernel
        out_specs = pl.BlockSpec((None, rows, columns), lambda j, order: (j, 0, 0))
        out_shape = jax.ShapeDtypeStruct((count, rows, columns), jnp.bfloat16)
    return pl.pallas_call(
        kernel,
        grid_spec=pltpu.PrefetchScalarGridSpec(
            num_scalar_prefetch=1,
            grid=(count,),
            in_specs=[
                pl.BlockSpec((rows, depth), lambda j, order: (0, 0)),
                pl.BlockSpec((depth, columns), lambda j, order: (0, order[j])),
            ],
            out_specs=out_specs,
        ),
        out_shape=out_shape,
        compiler_params=pltpu.CompilerParams(vmem_limit_bytes=VMEM),
        cost_estimate=QUICK,
        name="shares",
    )(order, attended, weight)


def add_kernel(total_ref, share_ref, out_ref):
    out_ref[...] = (total_ref[...].astype(jnp.float32) + share_ref[...].astype(jnp.float32)).astype(out_ref.dtype)


def add_share(total, others, hop, index, dtype):
    rows, columns = total.shape
    return pl.pallas_call(
        add_kernel,
        grid=(1,),
        in_specs=[
            pl.BlockSpec((rows, columns), lambda j: (0, 0)),
            pl.BlockSpec((None, rows, columns), lambda j: (hop, index, 0)),
        ],
        out_specs=pl.BlockSpec((rows, columns), lambda j: (0, 0)),
        out_shape=jax.ShapeDtypeStruct((rows, columns), dtype),
        compiler_params=pltpu.CompilerParams(vmem_limit_bytes=VMEM),
        cost_estimate=QUICK,
        name="add_share",
    )(total, others)


def turn_kernel(full_width, leaves_ref, total_ref, share_ref, latent_ref, fresh_ref, rows_ref, out_ref, sums_ref):
    total = total_ref[...].astype(jnp.float32) + share_ref[...].astype(jnp.float32)
    latent = latent_ref[...]
    advanced = latent + rows_ref[1:2, :] * (latent + rows_ref[0:1, :] * total)
    kept = jnp.where(leaves_ref[0] != 0, fresh_ref[...], advanced)
    out_ref[...] = kept
    lane = lax.broadcasted_iota(jnp.int32, (kept.shape[0], 128), 1)
    first = jnp.sum(kept, axis=1, keepdims=True)
    second = jnp.sum(kept * kept, axis=1, keepdims=True)
    both = jnp.where(lane == 0, first, jnp.where(lane == 1, second, 0.0))
    sums_ref[...] = jnp.transpose(both)[: sums_ref.shape[0]]


def turn(total, others, hop, index, latent, fresh, rows, leaves, full_width):
    height, columns = total.shape
    whole = pl.BlockSpec((height, columns), lambda j, leaves: (0, 0))
    return pl.pallas_call(
        functools.partial(turn_kernel, full_width),
        grid_spec=pltpu.PrefetchScalarGridSpec(
            num_scalar_prefetch=1,
            grid=(1,),
            in_specs=[
                whole,
                pl.BlockSpec((None, height, columns), lambda j, leaves: (hop, index, 0)),
                pl.BlockSpec((height, columns), lambda j, leaves: (index, 0)),
                pl.BlockSpec((height, columns), lambda j, leaves: (index, 0)),
                pl.BlockSpec((2, columns), lambda j, leaves: (0, 0)),
            ],
            out_specs=[whole, pl.BlockSpec((8, height), lambda j, leaves: (0, 0))],
        ),
        out_shape=[
            jax.ShapeDtypeStruct((height, columns), jnp.float32),
            jax.ShapeDtypeStruct((8, height), jnp.float32),
        ],
        compiler_params=pltpu.CompilerParams(vmem_limit_bytes=VMEM),
        cost_estimate=QUICK,
        name="turn",
    )(leaves, total, others, latent, fresh, rows)


def normalize_kernel(full_width, count, block_ref, rows_ref, *refs):
    sums = refs[0][...]
    for part in range(1, count):
        sums = sums + refs[part][...]
    upright = jnp.transpose(sums)
    mean = upright[:, 0:1] / full_width
    var = upright[:, 1:2] / full_width - mean * mean
    out_ref = refs[count]
    out_ref[...] = (
        (block_ref[...] - mean) * lax.rsqrt(var + epsilon) * (1.0 + rows_ref[1:2, :]) + rows_ref[0:1, :]
    ).astype(out_ref.dtype)


def normalize_turned(block, sums, rows, full_width):
    size = lax.axis_size("tensor")
    everyone = [sums]
    for distance in range(1, size):
        everyone.append(permute(sums, "tensor", lambda i: (i + distance) % size))
    return pl.pallas_call(
        functools.partial(normalize_kernel, full_width, size),
        out_shape=jax.ShapeDtypeStruct(block.shape, jnp.bfloat16),
        compiler_params=pltpu.CompilerParams(vmem_limit_bytes=VMEM),
        cost_estimate=QUICK,
        name="normalize",
    )(block, rows, *everyone)


def onward(block):
    size = lax.axis_size("frame")
    return permute(block, "frame", lambda i: (i + 1) % size)


def summed(block):
    size = lax.axis_size("tensor")
    total = block
    for distance in range(1, size):
        total = total + permute(block, "tensor", lambda i: (i + distance) % size)
    return total


def sums_of(block):
    return jnp.stack([jnp.sum(block, axis=1), jnp.sum(block * block, axis=1)])


def chunk_sums(sums, index, height):
    return sums[:, index * height : (index + 1) * height]


def normalize(block, sums, full_width, shift, scale):
    mean = sums[0] / full_width
    var = sums[1] / full_width - mean * mean
    return (
        (block - mean[:, None]) * lax.rsqrt(var + epsilon)[:, None] * (1.0 + scale) + shift
    ).astype(jnp.bfloat16)


def sibling(block):
    return permute(block, "frame", lambda i: i ^ 1)


def halo(pair):
    return dict(
        own=pair,
        across=permute(pair, "frame", lambda i: i ^ 2),
        third=permute(pair, "frame", lambda i: i + (3 if i % 2 else -3)),
    )


def halo_second(held):
    held["second"] = permute(held["across"], "frame", lambda i: i + (QUAD if i % QUAD < 2 else -QUAD))


def halo_sibling(held):
    held["sibling"] = sibling(jnp.concatenate([held["own"], held["across"], held["second"]]))


SIBLING = dict(near=0, beyond=1, other=2)


def tie(*arrays):
    return lax.optimization_barrier(arrays)


SOURCES = ("own", "near", "across", "beyond", "third", "second", "other")


def usable_sources(slot, frames, reach):
    place = slot % QUAD
    held = dict(
        own=slot,
        near=slot ^ 1,
        across=slot ^ 2,
        beyond=slot ^ 3,
        third=jnp.where(place % 2 == 0, slot - 3, slot + 3),
        second=jnp.where(place < 2, slot - 2, slot + 2),
        other=slot + jnp.where(place == 0, -1, jnp.where(place == 1, -3, jnp.where(place == 2, 3, 1))),
    )
    held = jnp.stack([jnp.asarray(held[name], jnp.int32) for name in SOURCES])
    return ((jnp.abs(held - slot) <= reach) & (held >= 0) & (held < frames)).astype(jnp.int32)


def on_device(
    queue_state,
    fresh_noise,
    levels,
    reach_slot,
    mod_table,
    step_table,
    norm_gain,
    input_weight,
    output_weight,
):
    rows, columns = queue_state.shape
    tensor_count = lax.axis_size("tensor")
    full_width = columns * tensor_count
    frames = lax.axis_size("frame")
    slot = lax.axis_index("frame")
    place = lax.axis_index("tensor")
    head_dim = norm_gain.shape[1]
    height = rows // CHUNKS

    def pieces_of(vector_level):
        row = lax.dynamic_index_in_dim(mod_table, vector_level, 0, keepdims=False)
        return [
            lax.dynamic_slice_in_dim(row, part * full_width + place * columns, columns) for part in range(3)
        ]

    level = levels[0]
    shift, scale, gate = pieces_of(level)
    step_size = lax.dynamic_index_in_dim(step_table, level, 0, keepdims=False)
    next_level = permute(levels, "frame", lambda i: (i - 1) % frames)[0]
    next_rows = jnp.stack(pieces_of(next_level)[:2])
    update_rows = jnp.stack([gate, jnp.full_like(gate, step_size)])
    leaves = (slot == frames - 1).astype(jnp.int32).reshape(1)
    usable = usable_sources(slot, frames, reach_slot[0])
    gather_order = (place - jnp.arange(tensor_count, dtype=jnp.int32)) % tensor_count
    scatter_order = (place - 1 - jnp.arange(tensor_count, dtype=jnp.int32)) % tensor_count
    weights = jnp.transpose(input_weight, (1, 0, 2))

    def chunk(array, index):
        return array[index * height : (index + 1) * height]

    first_sums = summed(sums_of(queue_state))
    normed = [
        normalize(chunk(queue_state, i), chunk_sums(first_sums, i, height), full_width, shift, scale)
        for i in range(CHUNKS)
    ]
    latents = None
    kept = None

    for step_number in range(STEPS):
        queries, sources = [], []
        gathered = [normed[0]]
        for _ in range(tensor_count - 2):
            gathered.append(ring(gathered[-1]))
        for i in range(CHUNKS):
            if i > 0:
                gathered[-1], sources[-1]["own"] = tie(gathered[-1], sources[-1]["own"])
            following = None
            if i + 1 < CHUNKS:
                gathered[-1], own = tie(gathered[-1], normed[i + 1])
                last, arrived = tie(ring(gathered[-1]), ring(own))
                following = [own, arrived]
                for _ in range(tensor_count - 3):
                    following.append(ring(following[-1]))
            else:
                last = ring(gathered[-1])
            if i > 1:
                last, sources[-2]["second"] = tie(last, sources[-2]["second"])
                halo_sibling(sources[-2])
            if 0 < i < CHUNKS - 1:
                last, sources[-1]["across"] = tie(last, sources[-1]["across"])
                halo_second(sources[-1])
            query, pair = project(gathered + [last], weights, gather_order, norm_gain)
            queries.append(query)
            sources.append(halo(pair))
            gathered = following
        final = CHUNKS - 1
        early = [(i, name) for i in range(final - 1) for name in SOURCES]
        early += [(final - 1, name) for name in ("own", "across", "third")] + [(final, "own")]
        middle = [(final - 1, "second"), (final, "across"), (final, "third")]
        middle += [(final - 1, name) for name in SIBLING]
        late = [(final, "second")] + [(final, name) for name in SIBLING]

        def absorb(names, running, last):
            return attend(
                queries,
                [sources[i]["sibling" if name in SIBLING else name] for i, name in names],
                [SIBLING.get(name, 0) for _, name in names],
                [SOURCES.index(name) for _, name in names],
                usable,
                running,
                last,
                head_dim,
            )

        before, after = sources[-2], sources[-1]
        queries[-1], before["across"] = tie(queries[-1], before["across"])
        halo_second(before)
        running = absorb(early, None, False)
        running, before["second"], after["across"], after["third"] = tie(
            running, before["second"], after["across"], after["third"]
        )
        halo_second(after)
        halo_sibling(before)
        running = absorb(middle, running, False)
        running, after["second"] = tie(running, after["second"])
        halo_sibling(after)
        running = absorb(late, running, True)

        if step_number > 0:
            kept, running = tie(kept, running)
            latents = [onward(block) for block in kept]

        totals = list(shares(running, output_weight, scatter_order[:1], CHUNKS))
        others = shares(running, output_weight, scatter_order[1:], 0)
        turning = step_number < STEPS - 1
        for hop in range(tensor_count - 1):
            last = hop == tensor_count - 2
            for j in range(CHUNKS):
                totals[j] = ring(totals[j])
                if not (last and turning):
                    totals[j] = add_share(totals[j], others, hop, j, jnp.float32 if last else jnp.bfloat16)
        if turning:
            kept, normed = [], []
            for j in range(CHUNKS):
                block, sums = turn(
                    totals[j],
                    others,
                    tensor_count - 2,
                    j,
                    queue_state,
                    fresh_noise,
                    update_rows,
                    leaves,
                    full_width,
                )
                kept.append(block)
                normed.append(onward(normalize_turned(block, sums, next_rows, full_width)))
    advanced = [latents[j] + step_size * (latents[j] + gate * totals[j]) for j in range(CHUNKS)]
    return jnp.concatenate(advanced, axis=0)


def solution(mesh):
    return jax.shard_map(
        on_device,
        mesh=mesh,
        in_specs=(
            P("frame", "tensor"),
            P(None, "tensor"),
            P("frame"),
            P("frame"),
            P(),
            P(),
            P(),
            P(None, None, "tensor"),
            P("tensor", None),
        ),
        out_specs=P("frame", "tensor"),
        check_vma=False,
    )
```

```python
import functools
import math

import jax
import jax.numpy as jnp
from jax import lax
from jax.experimental import pallas as pl
from jax.experimental.pallas import tpu as pltpu
from jax.sharding import PartitionSpec as P

STEPS = 2
QUAD = 4
CHUNKS = 3
TILE = 256
VMEM = 56 * 1024 * 1024

epsilon = 1e-06
QUICK = pl.CostEstimate(flops=1000, bytes_accessed=1000, transcendentals=0)


def permute(block, axis, route):
    size = lax.axis_size(axis)
    pairs = [(i, j) for i, j in ((i, route(i)) for i in range(size)) if 0 <= j < size]
    return lax.ppermute(block, axis, pairs)


def ring(block):
    size = lax.axis_size("tensor")
    return permute(block, "tensor", lambda i: (i + 1) % size)


def qkv_kernel(parts, heads, head_dim, order_ref, gain_ref, *refs):
    inputs, weights = refs[:parts], refs[parts : 2 * parts]
    query_ref, pair_ref = refs[2 * parts :]
    step = pl.program_id(0)
    total = jnp.dot(inputs[0][...], weights[0][...], preferred_element_type=jnp.float32)
    for part in range(1, parts):
        total += jnp.dot(inputs[part][...], weights[part][...], preferred_element_type=jnp.float32)

    def normed(row, factor):
        pieces = []
        for head in range(heads):
            piece = total[:, head * head_dim : (head + 1) * head_dim]
            scale = lax.rsqrt(jnp.mean(piece * piece, axis=-1, keepdims=True) + epsilon)
            pieces.append((piece * scale * (gain_ref[row : row + 1, :] * factor)).astype(jnp.bfloat16))
        return jnp.concatenate(pieces, axis=1) if heads > 1 else pieces[0]

    @pl.when(step == 0)
    def _():
        pair_ref[...] = normed(1, 1.0)

    @pl.when(step == 1)
    def _():
        pair_ref[...] = total.astype(jnp.bfloat16)

    @pl.when(step == 2)
    def _():
        query_ref[...] = normed(0, math.log2(math.e) / math.sqrt(head_dim))


def project(inputs, weight, order, norm_gain):
    parts = len(inputs)
    rows, columns = inputs[0].shape
    head_dim = norm_gain.shape[1]

    def weight_spec(part):
        return pl.BlockSpec((None, columns, columns), lambda j, order: ((j + 1) % 3, order[part], 0))

    return pl.pallas_call(
        functools.partial(qkv_kernel, parts, columns // head_dim, head_dim),
        grid_spec=pltpu.PrefetchScalarGridSpec(
            num_scalar_prefetch=1,
            grid=(3,),
            in_specs=[pl.BlockSpec(norm_gain.shape, lambda j, order: (0, 0))]
            + [pl.BlockSpec((rows, columns), lambda j, order: (0, 0)) for _ in range(parts)]
            + [weight_spec(part) for part in range(parts)],
            out_specs=[
                pl.BlockSpec((rows, columns), lambda j, order: (0, 0)),
                pl.BlockSpec((rows, columns), lambda j, order: (0, jnp.minimum(j, 1))),
            ],
        ),
        out_shape=[
            jax.ShapeDtypeStruct((rows, columns), jnp.bfloat16),
            jax.ShapeDtypeStruct((rows, 2 * columns), jnp.bfloat16),
        ],
        compiler_params=pltpu.CompilerParams(vmem_limit_bytes=VMEM),
        cost_estimate=QUICK,
        name="qkv",
    )(order, norm_gain, *inputs, *([weight] * parts))


def attend_kernel(chunks, marks, first, last, tile, usable_ref, *refs):
    pieces = len(marks)
    queries, refs = refs[:chunks], refs[chunks:]
    keys, values = refs[:pieces], refs[pieces : 2 * pieces]
    rest = refs[2 * pieces :]
    total_in = None
    if not first:
        total_in, rest = rest[0], rest[1:]
    (out_ref,) = rest
    height, head_dim = queries[0].shape
    wide = []
    for piece in range(pieces):
        value = values[piece][...]
        usable = usable_ref[marks[piece]].astype(jnp.float32).astype(value.dtype)
        wide.append(jnp.concatenate([value, jnp.ones_like(value)], axis=1) * usable)
    for chunk in range(chunks):
        for start in range(0, height, tile):
            query = queries[chunk][start : start + tile, :]
            at = pl.ds(chunk * height + start, tile)
            total = None if first else total_in[at, :]
            for piece in range(pieces):
                scores = lax.dot_general(
                    query, keys[piece][...], (((1,), (1,)), ((), ())), preferred_element_type=jnp.float32
                )
                probs = jnp.exp2(scores).astype(jnp.bfloat16)
                added = jnp.dot(probs, wide[piece], preferred_element_type=jnp.float32)
                total = added if total is None else total + added
            if last:
                out_ref[at, :] = (total[:, :head_dim] / total[:, head_dim:]).astype(out_ref.dtype)
            else:
                out_ref[at, :] = total


def attend(queries, blocks, parts, marks, usable, running, last, head_dim):
    height, columns = queries[0].shape
    chunks = len(queries)
    rows = height * chunks
    heads = columns // head_dim
    first = running is None
    tile = TILE if height % TILE == 0 else height

    def key_spec(part):
        return pl.BlockSpec((height, head_dim), lambda h, usable: (part, h))

    def value_spec(part):
        return pl.BlockSpec((height, head_dim), lambda h, usable: (part, heads + h))

    running_spec = pl.BlockSpec((None, rows, 2 * head_dim), lambda h, usable: (h, 0, 0))
    return pl.pallas_call(
        functools.partial(attend_kernel, chunks, marks, first, last, tile),
        grid_spec=pltpu.PrefetchScalarGridSpec(
            num_scalar_prefetch=1,
            grid=(heads,),
            in_specs=[pl.BlockSpec((height, head_dim), lambda h, usable: (0, h)) for _ in queries]
            + [key_spec(part) for part in parts]
            + [value_spec(part) for part in parts]
            + ([] if first else [running_spec]),
            out_specs=pl.BlockSpec((rows, head_dim), lambda h, usable: (0, h)) if last else running_spec,
        ),
        out_shape=jax.ShapeDtypeStruct((rows, columns), jnp.bfloat16)
        if last
        else jax.ShapeDtypeStruct((heads, rows, 2 * head_dim), jnp.float32),
        compiler_params=pltpu.CompilerParams(vmem_limit_bytes=VMEM),
        cost_estimate=QUICK,
        name="attend",
    )(usable, *queries, *blocks, *blocks, *([] if first else [running]))


def first_share_kernel(order_ref, attended_ref, weight_ref, *out_refs):
    share = jnp.dot(
        attended_ref[...], weight_ref[...], preferred_element_type=jnp.float32
    ).astype(jnp.bfloat16)
    height = out_refs[0].shape[0]
    for index, out_ref in enumerate(out_refs):
        out_ref[...] = share[index * height : (index + 1) * height]


def share_kernel(order_ref, attended_ref, weight_ref, out_ref):
    out_ref[...] = jnp.dot(
        attended_ref[...], weight_ref[...], preferred_element_type=jnp.float32
    ).astype(out_ref.dtype)


def shares(attended, weight, order, chunks):
    rows, depth = attended.shape
    count = order.shape[0]
    columns = weight.shape[1] // lax.axis_size("tensor")
    if chunks:
        kernel = first_share_kernel
        out_specs = [pl.BlockSpec((rows // chunks, columns), lambda j, order: (0, 0))] * chunks
        out_shape = [jax.ShapeDtypeStruct((rows // chunks, columns), jnp.bfloat16)] * chunks
    else:
        kernel = share_kernel
        out_specs = pl.BlockSpec((None, rows, columns), lambda j, order: (j, 0, 0))
        out_shape = jax.ShapeDtypeStruct((count, rows, columns), jnp.bfloat16)
    return pl.pallas_call(
        kernel,
        grid_spec=pltpu.PrefetchScalarGridSpec(
            num_scalar_prefetch=1,
            grid=(count,),
            in_specs=[
                pl.BlockSpec((rows, depth), lambda j, order: (0, 0)),
                pl.BlockSpec((depth, columns), lambda j, order: (0, order[j])),
            ],
            out_specs=out_specs,
        ),
        out_shape=out_shape,
        compiler_params=pltpu.CompilerParams(vmem_limit_bytes=VMEM),
        cost_estimate=QUICK,
        name="shares",
    )(order, attended, weight)


def add_kernel(total_ref, share_ref, out_ref):
    out_ref[...] = (total_ref[...].astype(jnp.float32) + share_ref[...].astype(jnp.float32)).astype(out_ref.dtype)


def add_share(total, others, hop, index, dtype):
    rows, columns = total.shape
    return pl.pallas_call(
        add_kernel,
        grid=(1,),
        in_specs=[
            pl.BlockSpec((rows, columns), lambda j: (0, 0)),
            pl.BlockSpec((None, rows, columns), lambda j: (hop, index, 0)),
        ],
        out_specs=pl.BlockSpec((rows, columns), lambda j: (0, 0)),
        out_shape=jax.ShapeDtypeStruct((rows, columns), dtype),
        compiler_params=pltpu.CompilerParams(vmem_limit_bytes=VMEM),
        cost_estimate=QUICK,
        name="add_share",
    )(total, others)


def turn_kernel(full_width, leaves_ref, total_ref, share_ref, latent_ref, fresh_ref, rows_ref, out_ref, sums_ref):
    total = total_ref[...].astype(jnp.float32) + share_ref[...].astype(jnp.float32)
    latent = latent_ref[...]
    advanced = latent + rows_ref[1:2, :] * (latent + rows_ref[0:1, :] * total)
    kept = jnp.where(leaves_ref[0] != 0, fresh_ref[...], advanced)
    out_ref[...] = kept
    lane = lax.broadcasted_iota(jnp.int32, (kept.shape[0], 128), 1)
    first = jnp.sum(kept, axis=1, keepdims=True)
    second = jnp.sum(kept * kept, axis=1, keepdims=True)
    both = jnp.where(lane == 0, first, jnp.where(lane == 1, second, 0.0))
    sums_ref[...] = jnp.transpose(both)[: sums_ref.shape[0]]


def turn(total, others, hop, index, latent, fresh, rows, leaves, full_width):
    height, columns = total.shape
    whole = pl.BlockSpec((height, columns), lambda j, leaves: (0, 0))
    return pl.pallas_call(
        functools.partial(turn_kernel, full_width),
        grid_spec=pltpu.PrefetchScalarGridSpec(
            num_scalar_prefetch=1,
            grid=(1,),
            in_specs=[
                whole,
                pl.BlockSpec((None, height, columns), lambda j, leaves: (hop, index, 0)),
                pl.BlockSpec((height, columns), lambda j, leaves: (index, 0)),
                pl.BlockSpec((height, columns), lambda j, leaves: (index, 0)),
                pl.BlockSpec((2, columns), lambda j, leaves: (0, 0)),
            ],
            out_specs=[whole, pl.BlockSpec((8, height), lambda j, leaves: (0, 0))],
        ),
        out_shape=[
            jax.ShapeDtypeStruct((height, columns), jnp.float32),
            jax.ShapeDtypeStruct((8, height), jnp.float32),
        ],
        compiler_params=pltpu.CompilerParams(vmem_limit_bytes=VMEM),
        cost_estimate=QUICK,
        name="turn",
    )(leaves, total, others, latent, fresh, rows)


def normalize_kernel(full_width, count, block_ref, rows_ref, *refs):
    sums = refs[0][...]
    for part in range(1, count):
        sums = sums + refs[part][...]
    upright = jnp.transpose(sums)
    mean = upright[:, 0:1] / full_width
    var = upright[:, 1:2] / full_width - mean * mean
    out_ref = refs[count]
    out_ref[...] = (
        (block_ref[...] - mean) * lax.rsqrt(var + epsilon) * (1.0 + rows_ref[1:2, :]) + rows_ref[0:1, :]
    ).astype(out_ref.dtype)


def normalize_turned(block, sums, rows, full_width):
    size = lax.axis_size("tensor")
    everyone = [sums]
    for distance in range(1, size):
        everyone.append(permute(sums, "tensor", lambda i: (i + distance) % size))
    return pl.pallas_call(
        functools.partial(normalize_kernel, full_width, size),
        out_shape=jax.ShapeDtypeStruct(block.shape, jnp.bfloat16),
        compiler_params=pltpu.CompilerParams(vmem_limit_bytes=VMEM),
        cost_estimate=QUICK,
        name="normalize",
    )(block, rows, *everyone)


def onward(block):
    size = lax.axis_size("frame")
    return permute(block, "frame", lambda i: (i + 1) % size)


def summed(block):
    size = lax.axis_size("tensor")
    total = block
    for distance in range(1, size):
        total = total + permute(block, "tensor", lambda i: (i + distance) % size)
    return total


def sums_of(block):
    return jnp.stack([jnp.sum(block, axis=1), jnp.sum(block * block, axis=1)])


def chunk_sums(sums, index, height):
    return sums[:, index * height : (index + 1) * height]


def normalize(block, sums, full_width, shift, scale):
    mean = sums[0] / full_width
    var = sums[1] / full_width - mean * mean
    return (
        (block - mean[:, None]) * lax.rsqrt(var + epsilon)[:, None] * (1.0 + scale) + shift
    ).astype(jnp.bfloat16)


def sibling(block):
    return permute(block, "frame", lambda i: i ^ 1)


def halo(pair):
    return dict(
        own=pair,
        across=permute(pair, "frame", lambda i: i ^ 2),
        third=permute(pair, "frame", lambda i: i + (3 if i % 2 else -3)),
    )


def halo_second(held):
    held["second"] = permute(held["across"], "frame", lambda i: i + (QUAD if i % QUAD < 2 else -QUAD))


def halo_sibling(held):
    held["sibling"] = sibling(jnp.concatenate([held["own"], held["across"], held["second"]]))


SIBLING = dict(near=0, beyond=1, other=2)


def tie(*arrays):
    return lax.optimization_barrier(arrays)


SOURCES = ("own", "near", "across", "beyond", "third", "second", "other")


def usable_sources(slot, frames, reach):
    place = slot % QUAD
    held = dict(
        own=slot,
        near=slot ^ 1,
        across=slot ^ 2,
        beyond=slot ^ 3,
        third=jnp.where(place % 2 == 0, slot - 3, slot + 3),
        second=jnp.where(place < 2, slot - 2, slot + 2),
        other=slot + jnp.where(place == 0, -1, jnp.where(place == 1, -3, jnp.where(place == 2, 3, 1))),
    )
    held = jnp.stack([jnp.asarray(held[name], jnp.int32) for name in SOURCES])
    return ((jnp.abs(held - slot) <= reach) & (held >= 0) & (held < frames)).astype(jnp.int32)


def on_device(
    queue_state,
    fresh_noise,
    levels,
    reach_slot,
    mod_table,
    step_table,
    norm_gain,
    input_weight,
    output_weight,
):
    rows, columns = queue_state.shape
    tensor_count = lax.axis_size("tensor")
    full_width = columns * tensor_count
    frames = lax.axis_size("frame")
    slot = lax.axis_index("frame")
    place = lax.axis_index("tensor")
    head_dim = norm_gain.shape[1]
    height = rows // CHUNKS

    def pieces_of(vector_level):
        row = lax.dynamic_index_in_dim(mod_table, vector_level, 0, keepdims=False)
        return [
            lax.dynamic_slice_in_dim(row, part * full_width + place * columns, columns) for part in range(3)
        ]

    level = levels[0]
    shift, scale, gate = pieces_of(level)
    step_size = lax.dynamic_index_in_dim(step_table, level, 0, keepdims=False)
    next_level = permute(levels, "frame", lambda i: (i - 1) % frames)[0]
    next_rows = jnp.stack(pieces_of(next_level)[:2])
    update_rows = jnp.stack([gate, jnp.full_like(gate, step_size)])
    leaves = (slot == frames - 1).astype(jnp.int32).reshape(1)
    usable = usable_sources(slot, frames, reach_slot[0])
    gather_order = (place - jnp.arange(tensor_count, dtype=jnp.int32)) % tensor_count
    scatter_order = (place - 1 - jnp.arange(tensor_count, dtype=jnp.int32)) % tensor_count
    weights = jnp.transpose(input_weight, (1, 0, 2))

    def chunk(array, index):
        return array[index * height : (index + 1) * height]

    first_sums = summed(sums_of(queue_state))
    normed = [
        normalize(chunk(queue_state, i), chunk_sums(first_sums, i, height), full_width, shift, scale)
        for i in range(CHUNKS)
    ]
    latents = None
    kept = None

    for step_number in range(STEPS):
        queries, sources = [], []
        gathered = [normed[0]]
        for _ in range(tensor_count - 2):
            gathered.append(ring(gathered[-1]))
        for i in range(CHUNKS):
            if i > 0:
                gathered[-1], sources[-1]["own"] = tie(gathered[-1], sources[-1]["own"])
            following = None
            if i + 1 < CHUNKS:
                gathered[-1], own = tie(gathered[-1], normed[i + 1])
                last, arrived = tie(ring(gathered[-1]), ring(own))
                following = [own, arrived]
                for _ in range(tensor_count - 3):
                    following.append(ring(following[-1]))
            else:
                last = ring(gathered[-1])
            if i > 1:
                last, sources[-2]["second"] = tie(last, sources[-2]["second"])
                halo_sibling(sources[-2])
            if 0 < i < CHUNKS - 1:
                last, sources[-1]["across"] = tie(last, sources[-1]["across"])
                halo_second(sources[-1])
            query, pair = project(gathered + [last], weights, gather_order, norm_gain)
            queries.append(query)
            sources.append(halo(pair))
            gathered = following
        final = CHUNKS - 1
        early = [(i, name) for i in range(final - 1) for name in SOURCES]
        early += [(final - 1, name) for name in ("own", "across", "third")] + [(final, "own")]
        middle = [(final - 1, "second"), (final, "across"), (final, "third")]
        middle += [(final - 1, name) for name in SIBLING]
        late = [(final, "second")] + [(final, name) for name in SIBLING]

        def absorb(names, running, last):
            return attend(
                queries,
                [sources[i]["sibling" if name in SIBLING else name] for i, name in names],
                [SIBLING.get(name, 0) for _, name in names],
                [SOURCES.index(name) for _, name in names],
                usable,
                running,
                last,
                head_dim,
            )

        before, after = sources[-2], sources[-1]
        queries[-1], before["across"] = tie(queries[-1], before["across"])
        halo_second(before)
        running = absorb(early, None, False)
        running, before["second"], after["across"], after["third"] = tie(
            running, before["second"], after["across"], after["third"]
        )
        halo_second(after)
        halo_sibling(before)
        running = absorb(middle, running, False)
        running, after["second"] = tie(running, after["second"])
        halo_sibling(after)
        running = absorb(late, running, True)

        if step_number > 0:
            kept, running = tie(kept, running)
            latents = [onward(block) for block in kept]

        totals = list(shares(running, output_weight, scatter_order[:1], CHUNKS))
        others = shares(running, output_weight, scatter_order[1:], 0)
        turning = step_number < STEPS - 1
        for hop in range(tensor_count - 1):
            last = hop == tensor_count - 2
            for j in range(CHUNKS):
                totals[j] = ring(totals[j])
                if not last:
                    totals[j] = add_share(totals[j], others, hop, j, jnp.bfloat16)
        if turning:
            kept, normed = [], []
            for j in range(CHUNKS):
                block, sums = turn(
                    totals[j],
                    others,
                    tensor_count - 2,
                    j,
                    queue_state,
                    fresh_noise,
                    update_rows,
                    leaves,
                    full_width,
                )
                kept.append(block)
                normed.append(onward(normalize_turned(block, sums, next_rows, full_width)))
    advanced = []
    for j in range(CHUNKS):
        total = totals[j].astype(jnp.float32) + chunk(others[tensor_count - 2], j).astype(jnp.float32)
        advanced.append(latents[j] + step_size * (latents[j] + gate * total))
    return jnp.concatenate(advanced, axis=0)


def solution(mesh):
    return jax.shard_map(
        on_device,
        mesh=mesh,
        in_specs=(
            P("frame", "tensor"),
            P(None, "tensor"),
            P("frame"),
            P("frame"),
            P(),
            P(),
            P(),
            P(None, None, "tensor"),
            P("tensor", None),
        ),
        out_specs=P("frame", "tensor"),
        check_vma=False,
    )
```
